512 devices in a mesh: replica: 64 (over z_lo, x, core), fsdp: 8 (over y, z_hi).
Axes of the slice: x: 4, y: 4, z: 16 (z_hi: 2, z_lo: 8; z = z_hi * 8 + z_lo), core: 2. Of those that a mesh axis runs over, the one named last changes fastest.
Arguments:
- hidden_in: bfloat16 [131072, 7168], P(('replica', 'fsdp')), may hold values from -6 to 6
- norm_gain: float32 [7168], replicated, may hold values from 0.5 to 1.5
- proj_weight: bfloat16 [7168, 512], P('fsdp'), may hold values from -0.0625 to 0.0625
- replica_params: bfloat16 [64, 7168, 512], P('replica', 'fsdp'), may hold values from -120 to 120, as said below
- outer_params: float32 [7168, 512], P(('fsdp', 'replica')), may hold values from -6 to 6
- momentum: float32 [7168, 512], P(('fsdp', 'replica')), may hold values from -6 to 6
Outputs:
- projected: bfloat16 [131072, 512], P(('replica', 'fsdp'))
- new_outer: float32 [7168, 512], P(('fsdp', 'replica'))
- new_momentum: float32 [7168, 512], P(('fsdp', 'replica'))
The draws below stay inside these ranges and needn't reach their ends.
Inputs may be any that keep to these rules, and one draw needn't show every extreme that they name: `replica_params`: finite values of varying size.
All inputs are finite; a program needn't handle non-finite values.
Results may differ from the reference program's by a relative error of at most 0.0049.
Values may be sent and summed in bfloat16 or wider, within the bound.
No kernel may reach another device: no remote copies, remote signals or barrier semaphores. Data moves between devices by JAX's collectives and lax.ppermute only.
A program may use at most 64 MiB of HBM per device.

```python
import math
import jax
import jax.numpy as jnp
from jax import lax

D = 7168
KA = 512
KV = 512
TOK_DEV = 256
TOKENS = 131072
N_REPLICA = 64


def draw_replica_params(key, part):
    key = jax.random.fold_in(key, 11)
    key_row, key_col, key_val = jax.random.split(key, 3)
    position = jnp.arange(D, dtype=jnp.float32) / (D - 1)
    row_scale = 3.0 ** position * jnp.exp(jax.random.uniform(key_row, (D,), jnp.float32, 0.0, math.log(4.0)))
    col_scale = jnp.exp(jax.random.uniform(key_col, (KV,), jnp.float32, 0.0, math.log(2.5)))
    scale = row_scale[:, None] * col_scale[None, :]
    values = jax.random.truncated_normal(key_val, -4.0, 4.0, (N_REPLICA, D, KV), jnp.float32)
    return (values * scale[None]).astype(jnp.bfloat16)


def shard_levels(own_key, dims, shards, smallest, top_value):
    level = 1.0
    for dim, shards_of in shards:
        heights = jax.random.uniform(jax.random.fold_in(jax.random.fold_in(own_key, 6), dim), (shards_of,), jnp.float32, smallest / len(shards), top_value / len(shards))
        level = level * jnp.repeat(jnp.exp(heights), dims[dim] // shards_of).reshape((-1,) + (1,) * (len(dims) - 1 - dim))
    return level


def bell_draw(own_key, shape, width, reach, cuts=(), held_as=jnp.bfloat16):
    level = shard_levels(own_key, shape, cuts, -0.22, 0.18) if cuts else 1.0
    values = jax.random.normal(own_key, shape, jnp.float32) * width * level
    return jnp.minimum(jnp.maximum(values, -reach), reach).astype(held_as)


def setup_inputs(seed: int = 0) -> dict:
    splits = jax.random.split(jax.random.key(seed), 7)
    hidden_in = bell_draw(splits[0], (TOKENS, D), 1.0, 6.0, ((0, 512),))
    norm_gain = jnp.clip(1.0 + 0.1 * jax.random.normal(splits[1], (D,), jnp.float32), 0.5, 1.5)
    proj_weight = bell_draw(splits[2], (D, KA), D ** -0.5, 0.0625, ((0, 8),))
    replica_params = draw_replica_params(jax.random.fold_in(splits[6], 71), 0)
    outer_params = bell_draw(splits[4], (D, KV), 1.0, 6.0, ((0, 512),), jnp.float32)
    momentum = bell_draw(splits[5], (D, KV), 0.5, 6.0, ((0, 512),), jnp.float32)
    return {"hidden_in": hidden_in, "norm_gain": norm_gain, "proj_weight": proj_weight, "replica_params": replica_params, "outer_params": outer_params, "momentum": momentum}


OUTER_LR = 0.7
MOMENTUM_DECAY = 0.9
CLIP_RATIO = 0.25

def reference(hidden_in, norm_gain, proj_weight, replica_params, outer_params, momentum):
    gain = norm_gain.astype(jnp.float32)

    def project(block):
        values = block.astype(jnp.float32)
        scaled = lax.rsqrt(lax.optimization_barrier(jnp.mean(values * values, axis=1, keepdims=True)) + 1e-05)
        normed = (values * scaled * gain).astype(jnp.bfloat16)
        return jnp.dot(normed, proj_weight, preferred_element_type=jnp.float32).astype(jnp.bfloat16)
    blocks = hidden_in.reshape(-1, TOK_DEV, D)
    projected = lax.map(project, blocks).reshape(-1, proj_weight.shape[1])

    def accumulate(total, params):
        return (total + params.astype(jnp.float32), None)
    summed, unused = lax.scan(accumulate, jnp.zeros(outer_params.shape, jnp.float32), replica_params)
    delta = outer_params - summed / N_REPLICA
    length = jnp.sqrt(jnp.sum(delta * delta))
    factor = jnp.minimum(1.0, CLIP_RATIO * jnp.sqrt(jnp.float32(D * KV)) / (length + 1e-06))
    clipped = factor * delta
    new_momentum = MOMENTUM_DECAY * momentum + clipped
    new_outer = outer_params - OUTER_LR * (clipped + MOMENTUM_DECAY * new_momentum)
    return (projected, new_outer, new_momentum)
```

```python
import functools

import jax
import jax.numpy as jnp
from jax import lax
from jax.experimental import pallas as pl
from jax.experimental.pallas import tpu as pltpu
from jax.sharding import Mesh, PartitionSpec as P

D = 7168
KV = 512

OUTER_LR = 0.7
MOMENTUM_DECAY = 0.9
CLIP_RATIO = 0.25

NAMES = ("z_lo", "x", "core", "y", "z_hi")
SIZES = (8, 4, 2, 4, 2)
N_REPLICA = 64
SHARE = 14
ROWS = 896
PIECE = 112
LANES = 128
F32 = jnp.float32
BF16 = jnp.bfloat16
VMEM = pl.BlockSpec(memory_space=pltpu.VMEM)
PARAMS = pltpu.CompilerParams(vmem_limit_bytes=48 * 1024 * 1024)


def call(body, name, out, n_in, scratch=()):
    many = isinstance(out, (tuple, list))
    return pl.pallas_call(
        body,
        name=name,
        out_shape=out,
        in_specs=[VMEM] * n_in,
        out_specs=[VMEM] * len(out) if many else VMEM,
        scratch_shapes=list(scratch),
        compiler_params=PARAMS,
    )


def regroup_body(src, out, wide, grouped):
    wide[...] = src[...].astype(F32)
    for xc in range(8):
        for z in range(8):
            first = PIECE * z + SHARE * xc
            grouped[xc, SHARE * z : SHARE * (z + 1), :] = wide[first : first + SHARE, :]
        out[xc] = grouped[xc].astype(BF16)


def first_sum_body(parts, out, total):
    total[...] = functools.reduce(lambda a, b: a + b, [parts[i].astype(F32) for i in range(8)])
    for z in range(8):
        for j in range(4):
            out[z, SHARE * j : SHARE * (j + 1), :] = total[SHARE * z : SHARE * (z + 1), LANES * j : LANES * (j + 1)]


def second_sum_body(parts, outer, delta, squares, total):
    total[...] = functools.reduce(lambda a, b: a + b, [parts[i] for i in range(8)])
    for j in range(4):
        cols = slice(LANES * j, LANES * (j + 1))
        delta[:, cols] = outer[:, cols] - total[SHARE * j : SHARE * (j + 1), :] / N_REPLICA
    d = delta[...]
    line = jnp.sum(d * d, axis=0, keepdims=True)
    line = line[:, :128] + line[:, 128:256] + line[:, 256:384] + line[:, 384:]
    squares[...] = jnp.broadcast_to(line[None], squares.shape)


def spread_sum_body(parts, out):
    out[...] = jnp.broadcast_to(jnp.sum(parts[...], axis=0, keepdims=True), out.shape)


def update_body(parts, delta, outer, momentum, new_outer, new_momentum):
    lanes = jnp.sum(parts[...], axis=0)[:1]
    length = jnp.sqrt(jnp.sum(lanes, axis=1, keepdims=True))
    limit = CLIP_RATIO * jnp.sqrt(jnp.full((1, 1), D * KV, F32))
    factor = jnp.minimum(1.0, limit / (length + 1e-06))
    clipped = factor * delta[...]
    moved = MOMENTUM_DECAY * momentum[...] + clipped
    new_momentum[...] = moved
    new_outer[...] = outer[...] - OUTER_LR * (clipped + MOMENTUM_DECAY * moved)


def norm_body(hidden, gain, out):
    values = hidden[...].astype(F32)
    scaled = lax.rsqrt(jnp.mean(values * values, axis=1, keepdims=True) + 1e-05)
    out[...] = (values * scaled * gain[...]).astype(BF16)


def norm(hidden, gain):
    rows, block = hidden.shape[0], 32
    return pl.pallas_call(
        norm_body,
        name="norm",
        grid=(rows // block,),
        out_shape=jax.ShapeDtypeStruct(hidden.shape, BF16),
        in_specs=[pl.BlockSpec((block, D), lambda i: (i, 0)), pl.BlockSpec((1, D), lambda i: (0, 0))],
        out_specs=pl.BlockSpec((block, D), lambda i: (i, 0)),
        compiler_params=PARAMS,
        cost_estimate=pl.CostEstimate(flops=5 * rows * D, bytes_accessed=4 * rows * D, transcendentals=rows),
    )(hidden, gain)


def project_body(half, left, right, own, other, out, total):
    @pl.when(pl.program_id(0) == 0)
    def _():
        total[...] = jnp.zeros_like(total)

    total[...] += jnp.dot(left[...], own[...], preferred_element_type=F32) + jnp.dot(
        right[...], other[...], preferred_element_type=F32
    )

    @pl.when(pl.program_id(0) == pl.num_programs(0) - 1)
    def _():
        out[...] = total[...].astype(BF16)


def project(half, normed, own, other):
    rows, cols = normed.shape[0], own.shape[1]
    return pl.pallas_call(
        project_body,
        name="project",
        out_shape=jax.ShapeDtypeStruct((rows, cols), BF16),
        grid_spec=pltpu.PrefetchScalarGridSpec(
            num_scalar_prefetch=1,
            grid=(4,),
            in_specs=[
                pl.BlockSpec((rows, ROWS), lambda y, h: (0, 2 * y + h[0])),
                pl.BlockSpec((rows, ROWS), lambda y, h: (0, 2 * y + 1 - h[0])),
                pl.BlockSpec((ROWS, cols), lambda y, h: (y, 0)),
                pl.BlockSpec((ROWS, cols), lambda y, h: (y, 0)),
            ],
            out_specs=pl.BlockSpec((rows, cols), lambda y, h: (0, 0)),
            scratch_shapes=[pltpu.VMEM((rows, cols), F32)],
        ),
        compiler_params=PARAMS,
        cost_estimate=pl.CostEstimate(
            flops=2 * rows * D * cols, bytes_accessed=2 * (D * cols + rows * D), transcendentals=0
        ),
    )(half, normed, normed, own, other)


def on_device(hidden_in, norm_gain, proj_weight, replica_params, outer_params, momentum):
    share = outer_params.shape
    f32 = lambda *dims: jax.ShapeDtypeStruct(dims, F32)
    grouped = call(
        regroup_body, "regroup", jax.ShapeDtypeStruct((8, PIECE, KV), BF16), 1,
        [pltpu.VMEM((ROWS, KV), F32), pltpu.VMEM((8, PIECE, KV), F32)],
    )(replica_params[0])
    grouped = lax.all_to_all(grouped, ("x", "core"), 0, 0)
    pieces = call(first_sum_body, "first_sum", f32(8, 56, LANES), 1, [pltpu.VMEM((PIECE, KV), F32)])(grouped)
    pieces = lax.all_to_all(pieces, "z_lo", 0, 0)
    delta, squares = call(
        second_sum_body, "second_sum", (f32(*share), f32(32, 8, LANES)), 2, [pltpu.VMEM((56, LANES), F32)]
    )(pieces, outer_params)
    squares = lax.all_to_all(squares, ("y", "x", "core"), 0, 0)
    squares = call(spread_sum_body, "spread_sum", f32(16, 8, LANES), 1)(squares)
    squares = lax.all_to_all(squares, ("z_lo", "z_hi"), 0, 0)
    new_outer, new_momentum = call(update_body, "update", (f32(*share), f32(*share)), 4)(
        squares, delta, outer_params, momentum
    )

    place = lax.axis_index("x") * 2 + lax.axis_index("core")
    half = lax.axis_index("z_hi")
    mine = lax.dynamic_slice_in_dim(proj_weight, place * PIECE, PIECE, 0)
    mirror = [(2 * z + h, 2 * (7 - z) + 1 - h) for z in range(8) for h in range(2)]
    theirs = lax.ppermute(mine, ("z_lo", "z_hi"), mirror)
    own = lax.all_gather(mine, ("y", "x", "core"), axis=0, tiled=True)
    other = lax.all_gather(theirs, ("y", "x", "core"), axis=0, tiled=True)
    normed = norm(hidden_in, norm_gain.reshape(1, -1))
    projected = project(half.astype(jnp.int32).reshape(1), normed, own, other)
    return (projected, new_outer, new_momentum)


def solution(mesh):
    inner = Mesh(mesh.devices.reshape(SIZES), NAMES)
    replica, fsdp = NAMES[:3], NAMES[3:]
    in_specs = (
        P(replica + fsdp, None),
        P(),
        P(fsdp, None),
        P(replica, fsdp, None),
        P(fsdp + replica, None),
        P(fsdp + replica, None),
    )
    out_specs = (
        P(replica + fsdp, None),
        P(fsdp + replica, None),
        P(fsdp + replica, None),
    )
    return jax.shard_map(
        on_device, mesh=inner, in_specs=in_specs, out_specs=out_specs, check_vma=False
    )
```

```python
import functools

import jax
import jax.numpy as jnp
from jax import lax
from jax.experimental import pallas as pl
from jax.experimental.pallas import tpu as pltpu
from jax.sharding import Mesh, PartitionSpec as P

D = 7168
KV = 512

OUTER_LR = 0.7
MOMENTUM_DECAY = 0.9
CLIP_RATIO = 0.25

NAMES = ("z_lo", "x", "core", "y", "z_hi")
SIZES = (8, 4, 2, 4, 2)
N_REPLICA = 64
SHARE = 14
ROWS = 896
PIECE = 112
LANES = 128
F32 = jnp.float32
BF16 = jnp.bfloat16
VMEM = pl.BlockSpec(memory_space=pltpu.VMEM)
PARAMS = pltpu.CompilerParams(vmem_limit_bytes=48 * 1024 * 1024)


LONG = pl.CostEstimate(flops=0, bytes_accessed=2**32, transcendentals=0)


def call(body, name, out, args, after=(), through=(), scratch=(), first=VMEM, cost=None):
    out = tuple(out) + tuple(jax.ShapeDtypeStruct(a.shape, a.dtype) for a in through)
    anywhere = pl.BlockSpec(memory_space=pl.ANY)
    given, kept = len(args) + len(after), len(out) - len(through)
    return pl.pallas_call(
        body,
        name=name,
        out_shape=out,
        in_specs=[first] + [VMEM] * (len(args) - 1) + [anywhere] * (len(after) + len(through)),
        out_specs=[VMEM] * kept + [anywhere] * len(through),
        scratch_shapes=list(scratch),
        input_output_aliases={given + i: kept + i for i in range(len(through))},
        compiler_params=PARAMS,
        cost_estimate=cost,
    )(*args, *after, *through)


def regroup_body(src, out, wide, grouped):
    wide[...] = src[...].astype(F32)
    for xc in range(8):
        for z in range(8):
            first = PIECE * z + SHARE * xc
            grouped[xc, SHARE * z : SHARE * (z + 1), :] = wide[first : first + SHARE, :]
        out[xc] = grouped[xc].astype(BF16)


def cut_body(place, weight, after, own, mine):
    rows, cols = mine.shape
    own[...] = weight[:, pl.ds(pl.multiple_of(place[0] * cols, cols), cols)]
    mine[...] = own[pl.ds(pl.multiple_of(place[1] * rows, rows), rows), :]


def first_sum_body(parts, *rest):
    out, total = rest[-2:]
    total[...] = functools.reduce(lambda a, b: a + b, [parts[i].astype(F32) for i in range(8)])
    for z in range(8):
        for j in range(4):
            out[z, SHARE * j : SHARE * (j + 1), :] = total[SHARE * z : SHARE * (z + 1), LANES * j : LANES * (j + 1)]


def lay_body(*refs):
    count = refs[-1].shape[0]
    for i in range(count):
        refs[-1][i] = refs[i][...]


def hold_body(given, after, out):
    out[...] = given[...]


def second_sum_body(parts, outer, *rest):
    delta, squares, total = rest[-3:]
    total[...] = functools.reduce(lambda a, b: a + b, [parts[i] for i in range(8)])
    for j in range(4):
        cols = slice(LANES * j, LANES * (j + 1))
        delta[:, cols] = outer[:, cols] - total[SHARE * j : SHARE * (j + 1), :] / N_REPLICA
    d = delta[...]
    line = jnp.sum(d * d, axis=0, keepdims=True)
    line = line[:, :128] + line[:, 128:256] + line[:, 256:384] + line[:, 384:]
    squares[...] = jnp.broadcast_to(line[None], squares.shape)


def spread_sum_body(parts, *rest):
    out = rest[-4]
    out[...] = jnp.broadcast_to(jnp.sum(parts[...], axis=0, keepdims=True), out.shape)


def update_body(parts, delta, outer, momentum, new_outer, new_momentum):
    lanes = jnp.sum(parts[...], axis=0)[:1]
    length = jnp.sqrt(jnp.sum(lanes, axis=1, keepdims=True))
    limit = CLIP_RATIO * jnp.sqrt(jnp.full((1, 1), D * KV, F32))
    factor = jnp.minimum(1.0, limit / (length + 1e-06))
    clipped = factor * delta[...]
    moved = MOMENTUM_DECAY * momentum[...] + clipped
    new_momentum[...] = moved
    new_outer[...] = outer[...] - OUTER_LR * (clipped + MOMENTUM_DECAY * moved)


def scale_body(hidden, after, out):
    squares = jnp.zeros((hidden.shape[0], LANES), F32)
    for first in range(0, D, LANES):
        values = hidden[:, first : first + LANES].astype(F32)
        squares += values * values
    scaled = lax.rsqrt(jnp.sum(squares, axis=1, keepdims=True) / D + 1e-05)
    out[...] = jnp.broadcast_to(scaled, out.shape)


def norm_body(hidden, gain, scaled, after, out):
    scale = scaled[...]
    for first in range(0, D, LANES):
        cols = slice(first, first + LANES)
        out[:, cols] = (hidden[:, cols].astype(F32) * scale * gain[:, cols]).astype(BF16)


def by_rows(body, name, width, dtype, hidden, args, after):
    rows, block = hidden.shape[0], 32
    return pl.pallas_call(
        body,
        name=name,
        grid=(rows // block,),
        out_shape=jax.ShapeDtypeStruct((rows, width), dtype),
        in_specs=[pl.BlockSpec((block, D), lambda i: (i, 0))]
        + [
            pl.BlockSpec((1, D), lambda i: (0, 0)) if a.shape[0] == 1 else pl.BlockSpec((block, a.shape[1]), lambda i: (i, 0))
            for a in args
        ]
        + [pl.BlockSpec(memory_space=pl.ANY)],
        out_specs=pl.BlockSpec((block, width), lambda i: (i, 0)),
        compiler_params=PARAMS,
        cost_estimate=LONG,
    )(hidden, *args, after)


DOT = functools.partial(jnp.dot, preferred_element_type=F32)


def project_body(order, near_own, far_own, near_other, far_other, early, late, first, second, third, fourth, near, far, weights, near_sum, far_sum):
    step = pl.program_id(0)

    @pl.when(step == 0)
    def _():
        near_sum[...] = jnp.zeros_like(near_sum)
        far_sum[...] = jnp.zeros_like(far_sum)

    rows = first.shape[1]
    for k, piece in enumerate((first, second, third, fourth)):
        weights[pl.ds(pl.multiple_of(order[8 + k] * rows, rows), rows), :] = piece[0] if k < 2 else piece[0, 0]

    def add(own):
        near_sum[...] += DOT(near_own[...], own) + DOT(near_other[...], weights[...])
        far_sum[...] += DOT(far_own[...], own) + DOT(far_other[...], weights[...])

    pl.when(step < 2)(lambda: add(early[0]))
    pl.when(step >= 2)(lambda: add(late[0]))

    @pl.when(step == pl.num_programs(0) - 1)
    def _():
        near[...] = near_sum[...].astype(BF16)
        far[...] = far_sum[...].astype(BF16)


def project(order, normed, far_normed, early, late, quad, quad_next, quad_late):
    rows, cols = normed.shape[0], early.shape[2]
    out = jax.ShapeDtypeStruct((rows, cols), BF16)
    own = pl.BlockSpec((rows, ROWS), lambda j, o: (0, o[j]))
    other = pl.BlockSpec((rows, ROWS), lambda j, o: (0, o[4 + j]))
    whole = pl.BlockSpec((rows, cols), lambda j, o: (0, 0))
    piece = pl.BlockSpec((1, ROWS // 4, cols), lambda j, o: (j, 0, 0))
    return pl.pallas_call(
        project_body,
        name="project",
        out_shape=(out, out),
        grid_spec=pltpu.PrefetchScalarGridSpec(
            num_scalar_prefetch=1,
            grid=(4,),
            in_specs=[
                own, own, other, other,
                pl.BlockSpec((1, ROWS, cols), lambda j, o: (jnp.minimum(j, 1), 0, 0)),
                pl.BlockSpec((1, ROWS, cols), lambda j, o: (jnp.maximum(j - 2, 0), 0, 0)),
                piece, piece,
                pl.BlockSpec((1, 1, ROWS // 4, cols), lambda j, o: (0, j, 0, 0)),
                pl.BlockSpec((1, 1, ROWS // 4, cols), lambda j, o: (1, j, 0, 0)),
            ],
            out_specs=(whole, whole),
            scratch_shapes=[pltpu.VMEM((ROWS, cols), BF16)] + [pltpu.VMEM((rows, cols), F32)] * 2,
        ),
        compiler_params=PARAMS,
        cost_estimate=pl.CostEstimate(
            flops=4 * rows * D * cols, bytes_accessed=2 * (D * cols + 2 * rows * D), transcendentals=0
        ),
    )(order, normed, far_normed, normed, far_normed, early, late, quad, quad_next, quad_late, quad_late)


def join_body(core, near, far, out):
    cols = near.shape[1]

    @pl.when(core[0] == 0)
    def _():
        out[:, :cols] = near[...]
        out[:, cols:] = far[...]

    @pl.when(core[0] == 1)
    def _():
        out[:, :cols] = far[...]
        out[:, cols:] = near[...]


def join(core, near, far):
    rows, cols = near.shape
    return pl.pallas_call(
        join_body,
        name="join",
        out_shape=jax.ShapeDtypeStruct((rows, 2 * cols), BF16),
        in_specs=[pl.BlockSpec(memory_space=pltpu.SMEM), VMEM, VMEM],
        out_specs=VMEM,
        compiler_params=PARAMS,
    )(core, near, far)


def exchange(array, axis, second):
    flips = (3, 1) if second else (1, 3)
    names = tuple(name for name in NAMES if name in (axis, "core"))
    number = lambda i, c: 2 * i + c if names[1] == "core" else 4 * c + i
    pairs = [(number(i, c), number(i ^ flips[c], c)) for i in range(4) for c in range(2)]
    return lax.ppermute(array, names, pairs)


SHIFTS = (1, 3, 2)


def spread(array, axis):
    return [lax.ppermute(array, axis, [(i, (i + s) % 4) for i in range(4)]) for s in SHIFTS]


def order_of(place, core):
    near = place ^ (1 + 2 * core)
    return [place, near, near ^ 2, place ^ 2]


def on_device(hidden_in, norm_gain, proj_weight, replica_params, outer_params, momentum):
    share, rows, cols = outer_params.shape, proj_weight.shape[0], KV // 2
    array = lambda dtype, *dims: jax.ShapeDtypeStruct(dims, dtype)
    x, y, core, half = [lax.axis_index(name).astype(jnp.int32) for name in ("x", "y", "core", "z_hi")]
    swap = [(0, 1), (1, 0)]

    (grouped,) = call(
        regroup_body, "regroup", (array(BF16, 8, PIECE, KV),), (replica_params[0],),
        scratch=[pltpu.VMEM((ROWS, KV), F32), pltpu.VMEM((8, PIECE, KV), F32)],
    )
    own, mine = call(
        cut_body, "cut", (array(BF16, rows, cols), array(BF16, rows // 4, cols)),
        (jnp.stack([core, x]), proj_weight), (grouped,), first=pl.BlockSpec(memory_space=pltpu.SMEM),
    )
    grouped = lax.all_to_all(grouped, ("x", "core"), 0, 0)
    mirror = [(2 * z + h, 2 * (7 - z) + 1 - h) for z in range(8) for h in range(2)]
    other = lax.ppermute(mine, ("z_lo", "z_hi"), mirror)
    own_next = exchange(own, "y", False)
    (pieces,) = call(
        first_sum_body, "first_sum", (array(F32, 8, 56, LANES),), (grouped,), (own_next, other), scratch=[pltpu.VMEM((PIECE, KV), F32)]
    )
    pieces_in = lax.all_to_all(pieces, "z_lo", 0, 0)
    scaled = by_rows(scale_body, "scale", LANES, F32, hidden_in, (), pieces)
    (other,) = call(hold_body, "hold", (array(BF16, *other.shape),), (other,), (pieces,), cost=LONG)
    others = [other] + spread(other, "y")
    (early,) = call(lay_body, "pair", (array(BF16, 2, rows, cols),), (own, own_next), (pieces,), cost=LONG)
    late = exchange(early, "y", True)
    delta, squares = call(
        second_sum_body, "second_sum", (array(F32, *share), array(F32, 32, 8, LANES)),
        (pieces_in, outer_params), (*others[1:], late, scaled), (), [pltpu.VMEM((56, LANES), F32)],
    )
    squares = lax.all_to_all(squares, ("y", "x", "core"), 0, 0)
    (other,) = call(lay_body, "lay", (array(BF16, 4, rows // 4, cols),), tuple(others), (delta,), cost=LONG)
    other_next = exchange(other, "x", False)
    normed = by_rows(norm_body, "norm", D, BF16, hidden_in, (norm_gain.reshape(1, -1), scaled), delta)
    squares, normed, other, other_next = call(
        spread_sum_body, "spread_sum", (array(F32, 16, 8, LANES),), (squares,), (), (normed, other, other_next)
    )
    far_normed = lax.ppermute(normed, "core", swap)
    other_late = exchange(jnp.stack([other, other_next]), "x", True)
    squares = lax.all_to_all(squares, ("z_lo", "z_hi"), 0, 0)
    ys, other_ys, xs = order_of(y, core), [(y - s) % 4 for s in (0,) + SHIFTS], order_of(x, core)
    order = jnp.stack([2 * k + half for k in ys] + [2 * k + 1 - half for k in other_ys] + xs)
    near, far = project(order, normed, far_normed, early, late, other, other_next, other_late)
    far = lax.ppermute(far, "core", swap)
    new_outer, new_momentum = call(
        update_body, "update", (array(F32, *share), array(F32, *share)), (squares, delta, outer_params, momentum)
    )
    projected = join(core.reshape(1), near, far)
    return (projected, new_outer, new_momentum)


def solution(mesh):
    inner = Mesh(mesh.devices.reshape(SIZES), NAMES)
    replica, fsdp = NAMES[:3], NAMES[3:]
    in_specs = (
        P(replica + fsdp, None),
        P(),
        P(fsdp, None),
        P(replica, fsdp, None),
        P(fsdp + replica, None),
        P(fsdp + replica, None),
    )
    out_specs = (
        P(replica + fsdp, None),
        P(fsdp + replica, None),
        P(fsdp + replica, None),
    )
    return jax.shard_map(
        on_device, mesh=inner, in_specs=in_specs, out_specs=out_specs, check_vma=False
    )
```

```python
import functools

import jax
import jax.numpy as jnp
from jax import lax
from jax.experimental import pallas as pl
from jax.experimental.pallas import tpu as pltpu
from jax.sharding import Mesh, PartitionSpec as P

D = 7168
KV = 512

OUTER_LR = 0.7
MOMENTUM_DECAY = 0.9
CLIP_RATIO = 0.25

NAMES = ("z_lo", "x", "core", "y", "z_hi")
SIZES = (8, 4, 2, 4, 2)
N_REPLICA = 64
SHARE = 14
ROWS = 896
PIECE = 112
LANES = 128
F32 = jnp.float32
BF16 = jnp.bfloat16
VMEM = pl.BlockSpec(memory_space=pltpu.VMEM)
PARAMS = pltpu.CompilerParams(vmem_limit_bytes=20 * 1024 * 1024)


LONG = pl.CostEstimate(flops=0, bytes_accessed=2**32, transcendentals=0)
TOKEN = jax.ShapeDtypeStruct((8, LANES), F32)


def call(body, name, out, args, after=(), scratch=(), first=VMEM, cost=None, through=None):
    anywhere = pl.BlockSpec(memory_space=pl.ANY)
    out, out_specs, aliases = tuple(out), [VMEM] * len(out), {}
    if through is not None:
        after, aliases = (*after, through), {len(args) + len(after): len(out)}
        out, out_specs = (*out, jax.ShapeDtypeStruct(through.shape, through.dtype)), out_specs + [anywhere]
    return pl.pallas_call(
        body,
        name=name,
        out_shape=out,
        in_specs=[first] + [VMEM] * (len(args) - 1) + [anywhere] * len(after),
        out_specs=out_specs,
        scratch_shapes=list(scratch),
        input_output_aliases=aliases,
        compiler_params=PARAMS,
        cost_estimate=cost,
    )(*args, *after)


def regroup_body(src, out, token, wide, grouped):
    token[...] = jnp.zeros_like(token)
    wide[...] = src[...].astype(F32)
    for xc in range(8):
        for z in range(8):
            first = PIECE * z + SHARE * xc
            grouped[xc, SHARE * z : SHARE * (z + 1), :] = wide[first : first + SHARE, :]
        out[xc] = grouped[xc].astype(BF16)


def cut_body(place, weight, after, own, mine):
    rows, cols = mine.shape
    own[...] = weight[:, pl.ds(pl.multiple_of(place[0] * cols, cols), cols)]
    mine[...] = own[pl.ds(pl.multiple_of(place[1] * rows, rows), rows), :]


def first_sum_body(parts, *rest):
    out, token, total = rest[-3:]
    token[...] = jnp.zeros_like(token)
    total[...] = functools.reduce(lambda a, b: a + b, [parts[i].astype(F32) for i in range(8)])
    for z in range(8):
        for j in range(4):
            out[z, SHARE * j : SHARE * (j + 1), :] = total[SHARE * z : SHARE * (z + 1), LANES * j : LANES * (j + 1)]


def lay_body(*refs):
    count = refs[-1].shape[0]
    for i in range(count):
        refs[-1][i] = refs[i][...]


def hold_body(given, after, out):
    out[...] = given[...]


def second_sum_body(parts, outer, *rest):
    delta, squares, token, through, total = rest[-5:]
    token[...] = jnp.zeros_like(token)
    total[...] = functools.reduce(lambda a, b: a + b, [parts[i] for i in range(8)])
    for j in range(4):
        cols = slice(LANES * j, LANES * (j + 1))
        delta[:, cols] = outer[:, cols] - total[SHARE * j : SHARE * (j + 1), :] / N_REPLICA
    d = delta[...]
    line = jnp.sum(d * d, axis=0, keepdims=True)
    line = line[:, :128] + line[:, 128:256] + line[:, 256:384] + line[:, 384:]
    squares[...] = jnp.broadcast_to(line[None], squares.shape)


def spread_sum_body(parts, *rest):
    out, token = rest[-2:]
    token[...] = jnp.zeros_like(token)
    out[...] = jnp.broadcast_to(jnp.sum(parts[...], axis=0, keepdims=True), out.shape)


def update_body(parts, delta, outer, momentum, new_outer, new_momentum):
    lanes = jnp.sum(parts[...], axis=0)[:1]
    length = jnp.sqrt(jnp.sum(lanes, axis=1, keepdims=True))
    limit = CLIP_RATIO * jnp.sqrt(jnp.full((1, 1), D * KV, F32))
    factor = jnp.minimum(1.0, limit / (length + 1e-06))
    clipped = factor * delta[...]
    moved = MOMENTUM_DECAY * momentum[...] + clipped
    new_momentum[...] = moved
    new_outer[...] = outer[...] - OUTER_LR * (clipped + MOMENTUM_DECAY * moved)


def norm_body(hidden, gain, after, out):
    for top in range(0, hidden.shape[0], 16):
        rows = slice(top, top + 16)
        squares = jnp.zeros((16, LANES), F32)
        for first in range(0, D, LANES):
            values = hidden[rows, first : first + LANES].astype(F32)
            squares += values * values
        scaled = lax.rsqrt(jnp.sum(squares, axis=1, keepdims=True) / D + 1e-05)
        scaled = jnp.broadcast_to(scaled, (16, LANES))
        for first in range(0, D, LANES):
            cols = slice(first, first + LANES)
            out[rows, cols] = (hidden[rows, cols].astype(F32) * scaled * gain[:, cols]).astype(BF16)


def norm(hidden, gain, after):
    rows, block = hidden.shape[0], 64
    return pl.pallas_call(
        norm_body,
        name="norm",
        grid=(rows // block,),
        out_shape=jax.ShapeDtypeStruct(hidden.shape, BF16),
        in_specs=[
            pl.BlockSpec((block, D), lambda i: (i, 0)),
            pl.BlockSpec((1, D), lambda i: (0, 0)),
            pl.BlockSpec(memory_space=pl.ANY),
        ],
        out_specs=pl.BlockSpec((block, D), lambda i: (i, 0)),
        compiler_params=PARAMS,
        cost_estimate=LONG,
    )(hidden, gain, after)


DOT = functools.partial(jnp.dot, preferred_element_type=F32)


def blocks(tokens, weights, order, first):
    cols = lambda k: pl.ds(pl.multiple_of(order[first + k] * ROWS, ROWS), ROWS)
    return functools.reduce(lambda a, b: a + b, [DOT(tokens[:, cols(k)], w[...]) for k, w in enumerate(weights)])


def project_own_body(order, near_in, far_in, early, late, after, near, far):
    parts = [early.at[0], early.at[1], late.at[0], late.at[1]]
    near[...] = blocks(near_in, parts, order, 0)
    far[...] = blocks(far_in, parts, order, 0)


def project_other_body(order, near_in, far_in, quad, quad_next, quad_late, near_own, far_own, near, far, weights):
    rows = quad.shape[1]
    for k in range(4):
        place = pl.ds(pl.multiple_of(order[8 + k] * rows, rows), rows)
        for j in range(4):
            weights[j, place, :] = (quad[j], quad_next[j], quad_late[0, j], quad_late[1, j])[k]
    parts = [weights.at[j] for j in range(4)]
    near[...] = (near_own[...] + blocks(near_in, parts, order, 4)).astype(BF16)
    far[...] = (far_own[...] + blocks(far_in, parts, order, 4)).astype(BF16)


def join_body(core, near, far, out):
    cols = near.shape[1]

    @pl.when(core[0] == 0)
    def _():
        out[:, :cols] = near[...]
        out[:, cols:] = far[...]

    @pl.when(core[0] == 1)
    def _():
        out[:, :cols] = far[...]
        out[:, cols:] = near[...]


def join(core, near, far):
    rows, cols = near.shape
    return pl.pallas_call(
        join_body,
        name="join",
        out_shape=jax.ShapeDtypeStruct((rows, 2 * cols), BF16),
        in_specs=[pl.BlockSpec(memory_space=pltpu.SMEM), VMEM, VMEM],
        out_specs=VMEM,
        compiler_params=PARAMS,
    )(core, near, far)


def exchange(array, axis, second):
    flips = (3, 1) if second else (1, 3)
    names = tuple(name for name in NAMES if name in (axis, "core"))
    number = lambda i, c: 2 * i + c if names[1] == "core" else 4 * c + i
    pairs = [(number(i, c), number(i ^ flips[c], c)) for i in range(4) for c in range(2)]
    return lax.ppermute(array, names, pairs)


SHIFTS = (1, 3, 2)


def spread(array, axis):
    return [lax.ppermute(array, axis, [(i, (i + s) % 4) for i in range(4)]) for s in SHIFTS]


def order_of(place, core):
    near = place ^ (1 + 2 * core)
    return [place, near, near ^ 2, place ^ 2]


def on_device(hidden_in, norm_gain, proj_weight, replica_params, outer_params, momentum):
    share, rows, cols = outer_params.shape, proj_weight.shape[0], KV // 2
    array = lambda dtype, *dims: jax.ShapeDtypeStruct(dims, dtype)
    x, y, core, half = [lax.axis_index(name).astype(jnp.int32) for name in ("x", "y", "core", "z_hi")]
    swap = [(0, 1), (1, 0)]

    scalars = pl.BlockSpec(memory_space=pltpu.SMEM)
    grouped, token = call(
        regroup_body, "regroup", (array(BF16, 8, PIECE, KV), TOKEN), (replica_params[0],),
        scratch=[pltpu.VMEM((ROWS, KV), F32), pltpu.VMEM((8, PIECE, KV), F32)],
    )
    own, mine = call(
        cut_body, "cut", (array(BF16, rows, cols), array(BF16, rows // 4, cols)),
        (jnp.stack([core, x]), proj_weight), (token,), first=scalars,
    )
    grouped = lax.all_to_all(grouped, ("x", "core"), 0, 0)
    mirror = [(2 * z + h, 2 * (7 - z) + 1 - h) for z in range(8) for h in range(2)]
    other = lax.ppermute(mine, ("z_lo", "z_hi"), mirror)
    own_next = exchange(own, "y", False)
    pieces, token = call(
        first_sum_body, "first_sum", (array(F32, 8, 56, LANES), TOKEN), (grouped,), (other, own_next),
        scratch=[pltpu.VMEM((PIECE, KV), F32)],
    )
    pieces = lax.all_to_all(pieces, "z_lo", 0, 0)
    gain = norm_gain.reshape(1, -1)
    normed = norm(hidden_in, gain, token)
    (early,) = call(lay_body, "pair", (array(BF16, 2, rows, cols),), (own, own_next), (token,))
    late = exchange(early, "y", True)
    (other,) = call(hold_body, "hold", (array(BF16, *other.shape),), (other,), (token,), cost=LONG)
    others = [other] + spread(other, "y")
    delta, squares, token, normed = call(
        second_sum_body, "second_sum", (array(F32, *share), array(F32, 32, 8, LANES), TOKEN),
        (pieces, outer_params), others[1:], [pltpu.VMEM((56, LANES), F32)], through=normed,
    )
    squares = lax.all_to_all(squares, ("y", "x", "core"), 0, 0)
    ys, other_ys, xs = order_of(y, core), [(y - s) % 4 for s in (0,) + SHIFTS], order_of(x, core)
    order = jnp.stack([2 * k + half for k in ys] + [2 * k + 1 - half for k in other_ys] + xs)
    quad = call(lay_body, "lay", (array(BF16, 4, rows // 4, cols),), others, (token,), cost=LONG)[0]
    quad_next = exchange(quad, "x", False)
    far_normed = lax.ppermute(normed, "core", swap)
    tokens = normed.shape[0]
    squares, token = call(
        spread_sum_body, "spread_sum", (array(F32, 16, 8, LANES), TOKEN), (squares,), (quad_next,)
    )
    squares = lax.all_to_all(squares, ("z_lo", "z_hi"), 0, 0)
    quads = call(lay_body, "pair", (array(BF16, 2, 4, rows // 4, cols),), (quad, quad_next), (token,))[0]
    quad_late = exchange(quads, "x", True)
    near, far = call(
        project_own_body, "project_own", (array(F32, tokens, cols),) * 2, (order, normed, far_normed, early, late), (token,),
        first=scalars, cost=LONG,
    )
    near, far = call(
        project_other_body, "project_other", (array(BF16, tokens, cols),) * 2,
        (order, normed, far_normed, quad, quad_next, quad_late, near, far),
        first=scalars, scratch=[pltpu.VMEM((4, rows, cols), BF16)], cost=LONG,
    )
    far = lax.ppermute(far, "core", swap)
    new_outer, new_momentum = call(
        update_body, "update", (array(F32, *share), array(F32, *share)), (squares, delta, outer_params, momentum)
    )
    projected = join(core.reshape(1), near, far)
    return (projected, new_outer, new_momentum)


def solution(mesh):
    inner = Mesh(mesh.devices.reshape(SIZES), NAMES)
    replica, fsdp = NAMES[:3], NAMES[3:]
    in_specs = (
        P(replica + fsdp, None),
        P(),
        P(fsdp, None),
        P(replica, fsdp, None),
        P(fsdp + replica, None),
        P(fsdp + replica, None),
    )
    out_specs = (
        P(replica + fsdp, None),
        P(fsdp + replica, None),
        P(fsdp + replica, None),
    )
    return jax.shard_map(
        on_device, mesh=inner, in_specs=in_specs, out_specs=out_specs, check_vma=False
    )
```

```python
import functools

import jax
import jax.numpy as jnp
from jax import lax
from jax.experimental import pallas as pl
from jax.experimental.pallas import tpu as pltpu
from jax.sharding import Mesh, PartitionSpec as P

D = 7168
KV = 512

OUTER_LR = 0.7
MOMENTUM_DECAY = 0.9
CLIP_RATIO = 0.25

NAMES = ("z_lo", "x", "core", "y", "z_hi")
SIZES = (8, 4, 2, 4, 2)
N_REPLICA = 64
SHARE = 14
ROWS = 896
PIECE = 112
LANES = 128
F32 = jnp.float32
BF16 = jnp.bfloat16
VMEM = pl.BlockSpec(memory_space=pltpu.VMEM)
PARAMS = pltpu.CompilerParams(vmem_limit_bytes=20 * 1024 * 1024)


LONG = pl.CostEstimate(flops=0, bytes_accessed=2**32, transcendentals=0)
TOKEN = jax.ShapeDtypeStruct((8, LANES), F32)


def call(body, name, out, args, after=(), scratch=(), first=VMEM, cost=None, through=None):
    anywhere = pl.BlockSpec(memory_space=pl.ANY)
    out, out_specs, aliases = tuple(out), [VMEM] * len(out), {}
    if through is not None:
        after, aliases = (*after, through), {len(args) + len(after): len(out)}
        out, out_specs = (*out, jax.ShapeDtypeStruct(through.shape, through.dtype)), out_specs + [anywhere]
    return pl.pallas_call(
        body,
        name=name,
        out_shape=out,
        in_specs=[first] + [VMEM] * (len(args) - 1 + len(after) - len(aliases)) + [anywhere] * len(aliases),
        out_specs=out_specs,
        scratch_shapes=list(scratch),
        input_output_aliases=aliases,
        compiler_params=PARAMS,
        cost_estimate=cost,
    )(*args, *after)


def regroup_body(src, out, token, wide, grouped):
    token[...] = jnp.zeros_like(token)
    wide[...] = src[...].astype(F32)
    for xc in range(8):
        for z in range(8):
            first = PIECE * z + SHARE * xc
            grouped[xc, SHARE * z : SHARE * (z + 1), :] = wide[first : first + SHARE, :]
        out[xc] = grouped[xc].astype(BF16)


def cut_body(place, weight, after, own, mine):
    rows, cols = mine.shape
    own[...] = weight[:, pl.ds(pl.multiple_of(place[0] * cols, cols), cols)]
    mine[...] = own[pl.ds(pl.multiple_of(place[1] * rows, rows), rows), :]


def first_sum_body(parts, *rest):
    out, token, total = rest[-3:]
    token[...] = jnp.zeros_like(token)
    total[...] = functools.reduce(lambda a, b: a + b, [parts[i].astype(F32) for i in range(8)])
    for z in range(8):
        for j in range(4):
            out[z, SHARE * j : SHARE * (j + 1), :] = total[SHARE * z : SHARE * (z + 1), LANES * j : LANES * (j + 1)]


def lay_body(*refs):
    count = refs[-1].shape[0]
    for i in range(count):
        refs[-1][i] = refs[i][...]


def hold_body(given, after, out):
    out[...] = given[...]


def second_sum_body(parts, outer, *rest):
    delta, squares, token, through, total = rest[-5:]
    token[...] = jnp.zeros_like(token)
    total[...] = functools.reduce(lambda a, b: a + b, [parts[i] for i in range(8)])
    for j in range(4):
        cols = slice(LANES * j, LANES * (j + 1))
        delta[:, cols] = outer[:, cols] - total[SHARE * j : SHARE * (j + 1), :] / N_REPLICA
    d = delta[...]
    line = jnp.sum(d * d, axis=0, keepdims=True)
    line = line[:, :128] + line[:, 128:256] + line[:, 256:384] + line[:, 384:]
    squares[...] = jnp.broadcast_to(line[None], squares.shape)


def spread_sum_body(parts, *rest):
    out, token = rest[-2:]
    token[...] = jnp.zeros_like(token)
    out[...] = jnp.broadcast_to(jnp.sum(parts[...], axis=0, keepdims=True), out.shape)


def update_body(parts, delta, outer, momentum, new_outer, new_momentum):
    lanes = jnp.sum(parts[...], axis=0)[:1]
    length = jnp.sqrt(jnp.sum(lanes, axis=1, keepdims=True))
    limit = CLIP_RATIO * jnp.sqrt(jnp.full((1, 1), D * KV, F32))
    factor = jnp.minimum(1.0, limit / (length + 1e-06))
    clipped = factor * delta[...]
    moved = MOMENTUM_DECAY * momentum[...] + clipped
    new_momentum[...] = moved
    new_outer[...] = outer[...] - OUTER_LR * (clipped + MOMENTUM_DECAY * moved)


def norm_body(hidden, gain, after, out):
    for top in range(0, hidden.shape[0], 16):
        rows = slice(top, top + 16)
        squares = jnp.zeros((16, LANES), F32)
        for first in range(0, D, LANES):
            values = hidden[rows, first : first + LANES].astype(F32)
            squares += values * values
        scaled = lax.rsqrt(jnp.sum(squares, axis=1, keepdims=True) / D + 1e-05)
        scaled = jnp.broadcast_to(scaled, (16, LANES))
        for first in range(0, D, LANES):
            cols = slice(first, first + LANES)
            out[rows, cols] = (hidden[rows, cols].astype(F32) * scaled * gain[:, cols]).astype(BF16)


def norm(hidden, gain, after):
    rows, block = hidden.shape[0], 64
    return pl.pallas_call(
        norm_body,
        name="norm",
        grid=(rows // block,),
        out_shape=jax.ShapeDtypeStruct(hidden.shape, BF16),
        in_specs=[
            pl.BlockSpec((block, D), lambda i: (i, 0)),
            pl.BlockSpec((1, D), lambda i: (0, 0)),
            pl.BlockSpec(memory_space=pl.ANY),
        ],
        out_specs=pl.BlockSpec((block, D), lambda i: (i, 0)),
        compiler_params=PARAMS,
        cost_estimate=LONG,
    )(hidden, gain, after)


DOT = functools.partial(jnp.dot, preferred_element_type=F32)


def project_body(order, normed, far_normed, early, late, quad, quad_next, quad_late, near, far, held, weights, sums, arrived):
    copies = [
        [
            pltpu.make_async_copy(
                tokens.at[:, pl.ds(pl.multiple_of(order[k] * ROWS, ROWS), ROWS)], held.at[t, k], arrived.at[t, k]
            )
            for t, tokens in enumerate((normed, far_normed))
        ]
        for k in range(8)
    ]
    for pair in copies:
        for copy in pair:
            copy.start()
    rows = quad.shape[1]
    for k in range(4):
        place = pl.ds(pl.multiple_of(order[8 + k] * rows, rows), rows)
        for j in range(4):
            weights[j, place, :] = (quad[j], quad_next[j], quad_late[0, j], quad_late[1, j])[k]
    parts = [early.at[0], early.at[1], late.at[0], late.at[1]] + [weights.at[j] for j in range(4)]
    for k in range(8):
        for t in range(2):
            copies[k][t].wait()
            term = DOT(held[t, k], parts[k][...])
            sums[t] = term if k == 0 else sums[t] + term
    near[...] = sums[0].astype(BF16)
    far[...] = sums[1].astype(BF16)


def project(order, normed, far_normed, early, late, quad, quad_next, quad_late):
    rows, cols = normed.shape[0], early.shape[2]
    anywhere = pl.BlockSpec(memory_space=pl.ANY)
    return pl.pallas_call(
        project_body,
        name="project",
        out_shape=(jax.ShapeDtypeStruct((rows, cols), BF16),) * 2,
        in_specs=[pl.BlockSpec(memory_space=pltpu.SMEM), anywhere, anywhere] + [VMEM] * 5,
        out_specs=(VMEM, VMEM),
        scratch_shapes=[
            pltpu.VMEM((2, 8, rows, ROWS), BF16),
            pltpu.VMEM((4, ROWS, cols), BF16),
            pltpu.VMEM((2, rows, cols), F32),
            pltpu.SemaphoreType.DMA((2, 8)),
        ],
        compiler_params=PARAMS,
        cost_estimate=LONG,
    )(order, normed, far_normed, early, late, quad, quad_next, quad_late)


def join_body(core, near, far, out):
    cols = near.shape[1]

    @pl.when(core[0] == 0)
    def _():
        out[:, :cols] = near[...]
        out[:, cols:] = far[...]

    @pl.when(core[0] == 1)
    def _():
        out[:, :cols] = far[...]
        out[:, cols:] = near[...]


def join(core, near, far):
    rows, cols = near.shape
    return pl.pallas_call(
        join_body,
        name="join",
        out_shape=jax.ShapeDtypeStruct((rows, 2 * cols), BF16),
        in_specs=[pl.BlockSpec(memory_space=pltpu.SMEM), VMEM, VMEM],
        out_specs=VMEM,
        compiler_params=PARAMS,
    )(core, near, far)


def exchange(array, axis, second):
    flips = (3, 1) if second else (1, 3)
    names = tuple(name for name in NAMES if name in (axis, "core"))
    number = lambda i, c: 2 * i + c if names[1] == "core" else 4 * c + i
    pairs = [(number(i, c), number(i ^ flips[c], c)) for i in range(4) for c in range(2)]
    return lax.ppermute(array, names, pairs)


SHIFTS = (1, 3, 2)


def spread(array, axis):
    return [lax.ppermute(array, axis, [(i, (i + s) % 4) for i in range(4)]) for s in SHIFTS]


def order_of(place, core):
    near = place ^ (1 + 2 * core)
    return [place, near, near ^ 2, place ^ 2]


def on_device(hidden_in, norm_gain, proj_weight, replica_params, outer_params, momentum):
    share, rows, cols = outer_params.shape, proj_weight.shape[0], KV // 2
    array = lambda dtype, *dims: jax.ShapeDtypeStruct(dims, dtype)
    x, y, core, half = [lax.axis_index(name).astype(jnp.int32) for name in ("x", "y", "core", "z_hi")]
    swap = [(0, 1), (1, 0)]

    scalars = pl.BlockSpec(memory_space=pltpu.SMEM)
    grouped, token = call(
        regroup_body, "regroup", (array(BF16, 8, PIECE, KV), TOKEN), (replica_params[0],),
        scratch=[pltpu.VMEM((ROWS, KV), F32), pltpu.VMEM((8, PIECE, KV), F32)],
    )
    own, mine = call(
        cut_body, "cut", (array(BF16, rows, cols), array(BF16, rows // 4, cols)),
        (jnp.stack([core, x]), proj_weight), (token,), first=scalars,
    )
    grouped = lax.all_to_all(grouped, ("x", "core"), 0, 0)
    mirror = [(2 * z + h, 2 * (7 - z) + 1 - h) for z in range(8) for h in range(2)]
    other = lax.ppermute(mine, ("z_lo", "z_hi"), mirror)
    own_next = exchange(own, "y", False)
    pieces, token = call(
        first_sum_body, "first_sum", (array(F32, 8, 56, LANES), TOKEN), (grouped,), (other, own_next),
        scratch=[pltpu.VMEM((PIECE, KV), F32)],
    )
    pieces = lax.all_to_all(pieces, "z_lo", 0, 0)
    gain = norm_gain.reshape(1, -1)
    normed = norm(hidden_in, gain, token)
    (early,) = call(lay_body, "pair", (array(BF16, 2, rows, cols),), (own, own_next), (token,))
    late = exchange(early, "y", True)
    (other,) = call(hold_body, "hold", (array(BF16, *other.shape),), (other,), (token,), cost=LONG)
    others = [other] + spread(other, "y")
    delta, squares, token, normed = call(
        second_sum_body, "second_sum", (array(F32, *share), array(F32, 32, 8, LANES), TOKEN),
        (pieces, outer_params), others[1:], [pltpu.VMEM((56, LANES), F32)], through=normed,
    )
    squares = lax.all_to_all(squares, ("y", "x", "core"), 0, 0)
    ys, other_ys, xs = order_of(y, core), [(y - s) % 4 for s in (0,) + SHIFTS], order_of(x, core)
    order = jnp.stack([2 * k + half for k in ys] + [2 * k + 1 - half for k in other_ys] + xs)
    quad = call(lay_body, "lay", (array(BF16, 4, rows // 4, cols),), others, (token,), cost=LONG)[0]
    quad_next = exchange(quad, "x", False)
    far_normed = lax.ppermute(normed, "core", swap)
    squares, token = call(
        spread_sum_body, "spread_sum", (array(F32, 16, 8, LANES), TOKEN), (squares,), (quad_next,)
    )
    squares = lax.all_to_all(squares, ("z_lo", "z_hi"), 0, 0)
    quads = call(lay_body, "pair", (array(BF16, 2, 4, rows // 4, cols),), (quad, quad_next), (token,))[0]
    quad_late = exchange(quads, "x", True)
    near, far = project(order, normed, far_normed, early, late, quad, quad_next, quad_late)
    far = lax.ppermute(far, "core", swap)
    new_outer, new_momentum = call(
        update_body, "update", (array(F32, *share), array(F32, *share)), (squares, delta, outer_params, momentum)
    )
    projected = join(core.reshape(1), near, far)
    return (projected, new_outer, new_momentum)


def solution(mesh):
    inner = Mesh(mesh.devices.reshape(SIZES), NAMES)
    replica, fsdp = NAMES[:3], NAMES[3:]
    in_specs = (
        P(replica + fsdp, None),
        P(),
        P(fsdp, None),
        P(replica, fsdp, None),
        P(fsdp + replica, None),
        P(fsdp + replica, None),
    )
    out_specs = (
        P(replica + fsdp, None),
        P(fsdp + replica, None),
        P(fsdp + replica, None),
    )
    return jax.shard_map(
        on_device, mesh=inner, in_specs=in_specs, out_specs=out_specs, check_vma=False
    )
```

```python
import functools

import jax
import jax.numpy as jnp
from jax import lax
from jax.experimental import pallas as pl
from jax.experimental.pallas import tpu as pltpu
from jax.sharding import Mesh, PartitionSpec as P

D = 7168
KV = 512

OUTER_LR = 0.7
MOMENTUM_DECAY = 0.9
CLIP_RATIO = 0.25

NAMES = ("z_lo", "x", "core", "y", "z_hi")
SIZES = (8, 4, 2, 4, 2)
N_REPLICA = 64
SHARE = 14
ROWS = 896
PIECE = 112
LANES = 128
F32 = jnp.float32
BF16 = jnp.bfloat16
VMEM = pl.BlockSpec(memory_space=pltpu.VMEM)
PARAMS = pltpu.CompilerParams(vmem_limit_bytes=20 * 1024 * 1024)


LONG = pl.CostEstimate(flops=0, bytes_accessed=2**32, transcendentals=0)
TOKEN = jax.ShapeDtypeStruct((8, LANES), F32)


def call(body, name, out, args, after=(), scratch=(), first=VMEM, cost=None, through=None):
    anywhere = pl.BlockSpec(memory_space=pl.ANY)
    out, out_specs, aliases = tuple(out), [VMEM] * len(out), {}
    if through is not None:
        after, aliases = (*after, through), {len(args) + len(after): len(out)}
        out, out_specs = (*out, jax.ShapeDtypeStruct(through.shape, through.dtype)), out_specs + [anywhere]
    return pl.pallas_call(
        body,
        name=name,
        out_shape=out,
        in_specs=[first] + [VMEM] * (len(args) - 1 + len(after) - len(aliases)) + [anywhere] * len(aliases),
        out_specs=out_specs,
        scratch_shapes=list(scratch),
        input_output_aliases=aliases,
        compiler_params=PARAMS,
        cost_estimate=cost,
    )(*args, *after)


def regroup_body(src, out, token, wide, grouped):
    token[...] = jnp.zeros_like(token)
    wide[...] = src[...].astype(F32)
    for xc in range(8):
        for z in range(8):
            first = PIECE * z + SHARE * xc
            grouped[xc, SHARE * z : SHARE * (z + 1), :] = wide[first : first + SHARE, :]
        out[xc] = grouped[xc].astype(BF16)


def cut_body(place, weight, after, own, mine):
    rows, cols = mine.shape
    own[...] = weight[:, pl.ds(pl.multiple_of(place[0] * cols, cols), cols)]
    mine[...] = own[pl.ds(pl.multiple_of(place[1] * rows, rows), rows), :]


def first_sum_body(parts, *rest):
    out, token, total = rest[-3:]
    token[...] = jnp.zeros_like(token)
    total[...] = functools.reduce(lambda a, b: a + b, [parts[i].astype(F32) for i in range(8)])
    for z in range(8):
        for j in range(4):
            out[z, SHARE * j : SHARE * (j + 1), :] = total[SHARE * z : SHARE * (z + 1), LANES * j : LANES * (j + 1)]


def lay_body(*refs):
    count = refs[-1].shape[0]
    for i in range(count):
        refs[-1][i] = refs[i][...]


def hold_body(given, after, out):
    out[...] = given[...]


def second_sum_body(parts, outer, *rest):
    delta, squares, token, through, total = rest[-5:]
    token[...] = jnp.zeros_like(token)
    total[...] = functools.reduce(lambda a, b: a + b, [parts[i] for i in range(8)])
    for j in range(4):
        cols = slice(LANES * j, LANES * (j + 1))
        delta[:, cols] = outer[:, cols] - total[SHARE * j : SHARE * (j + 1), :] / N_REPLICA
    d = delta[...]
    line = jnp.sum(d * d, axis=0, keepdims=True)
    line = line[:, :128] + line[:, 128:256] + line[:, 256:384] + line[:, 384:]
    squares[...] = jnp.broadcast_to(line[None], squares.shape)


def spread_sum_body(parts, *rest):
    out, token = rest[-2:]
    token[...] = jnp.zeros_like(token)
    out[...] = jnp.broadcast_to(jnp.sum(parts[...], axis=0, keepdims=True), out.shape)


def update_body(parts, delta, outer, momentum, new_outer, new_momentum):
    lanes = jnp.sum(parts[...], axis=0)[:1]
    length = jnp.sqrt(jnp.sum(lanes, axis=1, keepdims=True))
    limit = CLIP_RATIO * jnp.sqrt(jnp.full((1, 1), D * KV, F32))
    factor = jnp.minimum(1.0, limit / (length + 1e-06))
    clipped = factor * delta[...]
    moved = MOMENTUM_DECAY * momentum[...] + clipped
    new_momentum[...] = moved
    new_outer[...] = outer[...] - OUTER_LR * (clipped + MOMENTUM_DECAY * moved)


def norm_body(hidden, gain, after, out):
    for top in range(0, hidden.shape[0], 16):
        rows = slice(top, top + 16)
        squares = jnp.zeros((16, LANES), F32)
        for first in range(0, D, LANES):
            values = hidden[rows, first : first + LANES].astype(F32)
            squares += values * values
        scaled = lax.rsqrt(jnp.sum(squares, axis=1, keepdims=True) / D + 1e-05)
        scaled = jnp.broadcast_to(scaled, (16, LANES))
        for first in range(0, D, LANES):
            cols = slice(first, first + LANES)
            out[rows, cols] = (hidden[rows, cols].astype(F32) * scaled * gain[:, cols]).astype(BF16)


def norm(hidden, gain, after):
    rows, block = hidden.shape[0], 64
    return pl.pallas_call(
        norm_body,
        name="norm",
        grid=(rows // block,),
        out_shape=jax.ShapeDtypeStruct(hidden.shape, BF16),
        in_specs=[
            pl.BlockSpec((block, D), lambda i: (i, 0)),
            pl.BlockSpec((1, D), lambda i: (0, 0)),
            pl.BlockSpec(memory_space=pl.ANY),
        ],
        out_specs=pl.BlockSpec((block, D), lambda i: (i, 0)),
        compiler_params=PARAMS,
        cost_estimate=LONG,
    )(hidden, gain, after)


DOT = functools.partial(jnp.dot, preferred_element_type=F32)


def blocks(tokens, weights):
    return functools.reduce(lambda a, b: a + b, [DOT(tokens[k], w[...]) for k, w in enumerate(weights)])


def project_own_body(order, normed, far_normed, early, late, token, sums, kept, held, arrived):
    count = normed.shape[0]
    copies = [
        pltpu.make_async_copy(
            tokens.at[:, pl.ds(pl.multiple_of(order[k] * ROWS, ROWS), ROWS)],
            (held if k < 4 else kept).at[k % 4, pl.ds(t * count, count)],
            arrived.at[t, k],
        )
        for k in range(8)
        for t, tokens in enumerate((normed, far_normed))
    ]
    for copy in copies:
        copy.start()
    for copy in copies[:8]:
        copy.wait()
    sums[...] = blocks(held, [early.at[0], early.at[1], late.at[0], late.at[1]])
    for copy in copies[8:]:
        copy.wait()


def project_own(order, normed, far_normed, early, late, token):
    count, cols = 2 * normed.shape[0], early.shape[2]
    anywhere = pl.BlockSpec(memory_space=pl.ANY)
    return pl.pallas_call(
        project_own_body,
        name="project_own",
        out_shape=(jax.ShapeDtypeStruct((count, cols), F32), jax.ShapeDtypeStruct((4, count, ROWS), BF16)),
        in_specs=[pl.BlockSpec(memory_space=pltpu.SMEM), anywhere, anywhere] + [VMEM] * 3,
        out_specs=(VMEM, VMEM),
        scratch_shapes=[pltpu.VMEM((4, count, ROWS), BF16), pltpu.SemaphoreType.DMA((2, 8))],
        compiler_params=PARAMS,
        cost_estimate=LONG,
    )(order, normed, far_normed, early, late, token)


def project_other_body(order, kept, quad, quad_next, quad_late, sums, near, far, weights):
    rows, count = quad.shape[1], near.shape[0]
    for k in range(4):
        place = pl.ds(pl.multiple_of(order[8 + k] * rows, rows), rows)
        for j in range(4):
            weights[j, place, :] = (quad[j], quad_next[j], quad_late[0, j], quad_late[1, j])[k]
    total = sums[...] + blocks(kept, [weights.at[j] for j in range(4)])
    near[...] = total[:count].astype(BF16)
    far[...] = total[count:].astype(BF16)


def join_body(core, near, far, out):
    cols = near.shape[1]

    @pl.when(core[0] == 0)
    def _():
        out[:, :cols] = near[...]
        out[:, cols:] = far[...]

    @pl.when(core[0] == 1)
    def _():
        out[:, :cols] = far[...]
        out[:, cols:] = near[...]


def join(core, near, far):
    rows, cols = near.shape
    return pl.pallas_call(
        join_body,
        name="join",
        out_shape=jax.ShapeDtypeStruct((rows, 2 * cols), BF16),
        in_specs=[pl.BlockSpec(memory_space=pltpu.SMEM), VMEM, VMEM],
        out_specs=VMEM,
        compiler_params=PARAMS,
    )(core, near, far)


def exchange(array, axis, second):
    flips = (3, 1) if second else (1, 3)
    names = tuple(name for name in NAMES if name in (axis, "core"))
    number = lambda i, c: 2 * i + c if names[1] == "core" else 4 * c + i
    pairs = [(number(i, c), number(i ^ flips[c], c)) for i in range(4) for c in range(2)]
    return lax.ppermute(array, names, pairs)


SHIFTS = (1, 3, 2)


def spread(array, axis):
    return [lax.ppermute(array, axis, [(i, (i + s) % 4) for i in range(4)]) for s in SHIFTS]


def order_of(place, core):
    near = place ^ (1 + 2 * core)
    return [place, near, near ^ 2, place ^ 2]


def on_device(hidden_in, norm_gain, proj_weight, replica_params, outer_params, momentum):
    share, rows, cols = outer_params.shape, proj_weight.shape[0], KV // 2
    array = lambda dtype, *dims: jax.ShapeDtypeStruct(dims, dtype)
    x, y, core, half = [lax.axis_index(name).astype(jnp.int32) for name in ("x", "y", "core", "z_hi")]
    swap = [(0, 1), (1, 0)]

    scalars = pl.BlockSpec(memory_space=pltpu.SMEM)
    grouped, token = call(
        regroup_body, "regroup", (array(BF16, 8, PIECE, KV), TOKEN), (replica_params[0],),
        scratch=[pltpu.VMEM((ROWS, KV), F32), pltpu.VMEM((8, PIECE, KV), F32)],
    )
    own, mine = call(
        cut_body, "cut", (array(BF16, rows, cols), array(BF16, rows // 4, cols)),
        (jnp.stack([core, x]), proj_weight), (token,), first=scalars,
    )
    grouped = lax.all_to_all(grouped, ("x", "core"), 0, 0)
    mirror = [(2 * z + h, 2 * (7 - z) + 1 - h) for z in range(8) for h in range(2)]
    other = lax.ppermute(mine, ("z_lo", "z_hi"), mirror)
    own_next = exchange(own, "y", False)
    pieces, token = call(
        first_sum_body, "first_sum", (array(F32, 8, 56, LANES), TOKEN), (grouped,), (other, own_next),
        scratch=[pltpu.VMEM((PIECE, KV), F32)],
    )
    pieces = lax.all_to_all(pieces, "z_lo", 0, 0)
    gain = norm_gain.reshape(1, -1)
    normed = norm(hidden_in, gain, token)
    (early,) = call(lay_body, "pair", (array(BF16, 2, rows, cols),), (own, own_next), (token,))
    late = exchange(early, "y", True)
    (other,) = call(hold_body, "hold", (array(BF16, *other.shape),), (other,), (token,), cost=LONG)
    others = [other] + spread(other, "y")
    delta, squares, token, normed = call(
        second_sum_body, "second_sum", (array(F32, *share), array(F32, 32, 8, LANES), TOKEN),
        (pieces, outer_params), others[1:], [pltpu.VMEM((56, LANES), F32)], through=normed,
    )
    squares = lax.all_to_all(squares, ("y", "x", "core"), 0, 0)
    ys, other_ys, xs = order_of(y, core), [(y - s) % 4 for s in (0,) + SHIFTS], order_of(x, core)
    order = jnp.stack([2 * k + half for k in ys] + [2 * k + 1 - half for k in other_ys] + xs)
    quad = call(lay_body, "lay", (array(BF16, 4, rows // 4, cols),), others, (token,), cost=LONG)[0]
    quad_next = exchange(quad, "x", False)
    far_normed = lax.ppermute(normed, "core", swap)
    squares, token = call(
        spread_sum_body, "spread_sum", (array(F32, 16, 8, LANES), TOKEN), (squares,), (quad_next,)
    )
    squares = lax.all_to_all(squares, ("z_lo", "z_hi"), 0, 0)
    quads = call(lay_body, "pair", (array(BF16, 2, 4, rows // 4, cols),), (quad, quad_next), (token,))[0]
    quad_late = exchange(quads, "x", True)
    sums, kept = project_own(order, normed, far_normed, early, late, token)
    near, far = call(
        project_other_body, "project_other", (array(BF16, normed.shape[0], cols),) * 2,
        (order, kept, quad, quad_next, quad_late, sums),
        first=scalars, scratch=[pltpu.VMEM((4, rows, cols), BF16)], cost=LONG,
    )
    far = lax.ppermute(far, "core", swap)
    new_outer, new_momentum = call(
        update_body, "update", (array(F32, *share), array(F32, *share)), (squares, delta, outer_params, momentum)
    )
    projected = join(core.reshape(1), near, far)
    return (projected, new_outer, new_momentum)


def solution(mesh):
    inner = Mesh(mesh.devices.reshape(SIZES), NAMES)
    replica, fsdp = NAMES[:3], NAMES[3:]
    in_specs = (
        P(replica + fsdp, None),
        P(),
        P(fsdp, None),
        P(replica, fsdp, None),
        P(fsdp + replica, None),
        P(fsdp + replica, None),
    )
    out_specs = (
        P(replica + fsdp, None),
        P(fsdp + replica, None),
        P(fsdp + replica, None),
    )
    return jax.shard_map(
        on_device, mesh=inner, in_specs=in_specs, out_specs=out_specs, check_vma=False
    )
```

```python
import functools

import jax
import jax.numpy as jnp
from jax import lax
from jax.experimental import pallas as pl
from jax.experimental.pallas import tpu as pltpu
from jax.sharding import Mesh, PartitionSpec as P

D = 7168
KV = 512

OUTER_LR = 0.7
MOMENTUM_DECAY = 0.9
CLIP_RATIO = 0.25

NAMES = ("z_lo", "x", "core", "y", "z_hi")
SIZES = (8, 4, 2, 4, 2)
N_REPLICA = 64
SHARE = 14
ROWS = 896
PIECE = 112
LANES = 128
F32 = jnp.float32
BF16 = jnp.bfloat16
VMEM = pl.BlockSpec(memory_space=pltpu.VMEM)
PARAMS = pltpu.CompilerParams(vmem_limit_bytes=20 * 1024 * 1024)


LONG = pl.CostEstimate(flops=0, bytes_accessed=2**32, transcendentals=0)
TOKEN = jax.ShapeDtypeStruct((8, LANES), F32)


def call(body, name, out, args, after=(), scratch=(), first=VMEM, cost=None, through=None):
    anywhere = pl.BlockSpec(memory_space=pl.ANY)
    out, out_specs, aliases = tuple(out), [VMEM] * len(out), {}
    if through is not None:
        after, aliases = (*after, through), {len(args) + len(after): len(out)}
        out, out_specs = (*out, jax.ShapeDtypeStruct(through.shape, through.dtype)), out_specs + [anywhere]
    return pl.pallas_call(
        body,
        name=name,
        out_shape=out,
        in_specs=[first] + [VMEM] * (len(args) - 1 + len(after) - len(aliases)) + [anywhere] * len(aliases),
        out_specs=out_specs,
        scratch_shapes=list(scratch),
        input_output_aliases=aliases,
        compiler_params=PARAMS,
        cost_estimate=cost,
    )(*args, *after)


def regroup_body(src, after, out, token, wide, grouped):
    token[...] = jnp.zeros_like(token)
    wide[...] = src[...].astype(F32)
    for xc in range(8):
        for z in range(8):
            first = PIECE * z + SHARE * xc
            grouped[xc, SHARE * z : SHARE * (z + 1), :] = wide[first : first + SHARE, :]
        out[xc] = grouped[xc].astype(BF16)


def cut_body(place, weight, own, mine):
    rows, cols = mine.shape
    own[...] = weight[:, pl.ds(pl.multiple_of(place[0] * cols, cols), cols)]
    mine[...] = own[pl.ds(pl.multiple_of(place[1] * rows, rows), rows), :]


def first_sum_body(parts, *rest):
    out, token, through, total = rest[-4:]
    token[...] = jnp.zeros_like(token)
    total[...] = functools.reduce(lambda a, b: a + b, [parts[i].astype(F32) for i in range(8)])
    for z in range(8):
        for j in range(4):
            out[z, SHARE * j : SHARE * (j + 1), :] = total[SHARE * z : SHARE * (z + 1), LANES * j : LANES * (j + 1)]


def lay_body(*refs):
    count = refs[-1].shape[0]
    for i in range(count):
        refs[-1][i] = refs[i][...]


def hold_body(given, after, out):
    out[...] = given[...]


def second_sum_body(parts, outer, *rest):
    delta, squares, token, through, total = rest[-5:]
    token[...] = jnp.zeros_like(token)
    total[...] = functools.reduce(lambda a, b: a + b, [parts[i] for i in range(8)])
    for j in range(4):
        cols = slice(LANES * j, LANES * (j + 1))
        delta[:, cols] = outer[:, cols] - total[SHARE * j : SHARE * (j + 1), :] / N_REPLICA
    d = delta[...]
    line = jnp.sum(d * d, axis=0, keepdims=True)
    line = line[:, :128] + line[:, 128:256] + line[:, 256:384] + line[:, 384:]
    squares[...] = jnp.broadcast_to(line[None], squares.shape)


def spread_sum_body(parts, *rest):
    out, token = rest[-2:]
    token[...] = jnp.zeros_like(token)
    out[...] = jnp.broadcast_to(jnp.sum(parts[...], axis=0, keepdims=True), out.shape)


def finish_body(core, parts, delta, outer, momentum, near, far, new_outer, new_momentum, projected):
    lanes = jnp.sum(parts[...], axis=0)[:1]
    length = jnp.sqrt(jnp.sum(lanes, axis=1, keepdims=True))
    limit = CLIP_RATIO * jnp.sqrt(jnp.full((1, 1), D * KV, F32))
    factor = jnp.minimum(1.0, limit / (length + 1e-06))
    clipped = factor * delta[...]
    moved = MOMENTUM_DECAY * momentum[...] + clipped
    new_momentum[...] = moved
    new_outer[...] = outer[...] - OUTER_LR * (clipped + MOMENTUM_DECAY * moved)
    cols = near.shape[1]
    for c in range(2):

        @pl.when(core[0] == c)
        def _(c=c):
            projected[:, c * cols : (c + 1) * cols] = near[...]
            projected[:, (1 - c) * cols : (2 - c) * cols] = far[...]


def norm_body(hidden, gain, after, out):
    for top in range(0, hidden.shape[0], 16):
        rows = slice(top, top + 16)
        squares = jnp.zeros((16, LANES), F32)
        for first in range(0, D, LANES):
            values = hidden[rows, first : first + LANES].astype(F32)
            squares += values * values
        scaled = lax.rsqrt(jnp.sum(squares, axis=1, keepdims=True) / D + 1e-05)
        scaled = jnp.broadcast_to(scaled, (16, LANES))
        for first in range(0, D, LANES):
            cols = slice(first, first + LANES)
            out[rows, cols] = (hidden[rows, cols].astype(F32) * scaled * gain[:, cols]).astype(BF16)


def norm(hidden, gain, after):
    rows, block = hidden.shape[0], 64
    return pl.pallas_call(
        norm_body,
        name="norm",
        grid=(rows // block,),
        out_shape=jax.ShapeDtypeStruct(hidden.shape, BF16),
        in_specs=[
            pl.BlockSpec((block, D), lambda i: (i, 0)),
            pl.BlockSpec((1, D), lambda i: (0, 0)),
            pl.BlockSpec(memory_space=pl.ANY),
        ],
        out_specs=pl.BlockSpec((block, D), lambda i: (i, 0)),
        compiler_params=PARAMS,
        cost_estimate=LONG,
    )(hidden, gain, after)


DOT = functools.partial(jnp.dot, preferred_element_type=F32)


def blocks(tokens, weights):
    return functools.reduce(lambda a, b: a + b, [DOT(tokens[k], w[...]) for k, w in enumerate(weights)])


def project_own_body(order, normed, far_normed, early, late, token, sums, kept, held, arrived):
    count = normed.shape[0]
    copies = [
        pltpu.make_async_copy(
            tokens.at[:, pl.ds(pl.multiple_of(order[k] * ROWS, ROWS), ROWS)],
            (held if k < 4 else kept).at[k % 4, pl.ds(t * count, count)],
            arrived.at[t, k],
        )
        for k in range(8)
        for t, tokens in enumerate((normed, far_normed))
    ]
    for copy in copies:
        copy.start()
    for copy in copies[:8]:
        copy.wait()
    sums[...] = blocks(held, [early.at[0], early.at[1], late.at[0], late.at[1]])
    for copy in copies[8:]:
        copy.wait()


def project_own(order, normed, far_normed, early, late, token):
    count, cols = 2 * normed.shape[0], early.shape[2]
    anywhere = pl.BlockSpec(memory_space=pl.ANY)
    return pl.pallas_call(
        project_own_body,
        name="project_own",
        out_shape=(jax.ShapeDtypeStruct((count, cols), F32), jax.ShapeDtypeStruct((4, count, ROWS), BF16)),
        in_specs=[pl.BlockSpec(memory_space=pltpu.SMEM), anywhere, anywhere] + [VMEM] * 3,
        out_specs=(VMEM, VMEM),
        scratch_shapes=[pltpu.VMEM((4, count, ROWS), BF16), pltpu.SemaphoreType.DMA((2, 8))],
        compiler_params=PARAMS,
        cost_estimate=LONG,
    )(order, normed, far_normed, early, late, token)


def project_other_body(order, kept, quad, quad_next, quad_late, sums, near, far, weights):
    rows, count = quad.shape[1], near.shape[0]
    for k in range(4):
        place = pl.ds(pl.multiple_of(order[8 + k] * rows, rows), rows)
        for j in range(4):
            weights[j, place, :] = (quad[j], quad_next[j], quad_late[0, j], quad_late[1, j])[k]
    total = sums[...] + blocks(kept, [weights.at[j] for j in range(4)])
    near[...] = total[:count].astype(BF16)
    far[...] = total[count:].astype(BF16)


def exchange(array, axis, second):
    flips = (3, 1) if second else (1, 3)
    names = tuple(name for name in NAMES if name in (axis, "core"))
    number = lambda i, c: 2 * i + c if names[1] == "core" else 4 * c + i
    pairs = [(number(i, c), number(i ^ flips[c], c)) for i in range(4) for c in range(2)]
    return lax.ppermute(array, names, pairs)


SHIFTS = (1, 3, 2)


def spread(array, axis):
    return [lax.ppermute(array, axis, [(i, (i + s) % 4) for i in range(4)]) for s in SHIFTS]


def order_of(place, core):
    near = place ^ (1 + 2 * core)
    return [place, near, near ^ 2, place ^ 2]


def on_device(hidden_in, norm_gain, proj_weight, replica_params, outer_params, momentum):
    share, rows, cols = outer_params.shape, proj_weight.shape[0], KV // 2
    array = lambda dtype, *dims: jax.ShapeDtypeStruct(dims, dtype)
    x, y, core, half = [lax.axis_index(name).astype(jnp.int32) for name in ("x", "y", "core", "z_hi")]
    swap = [(0, 1), (1, 0)]

    scalars = pl.BlockSpec(memory_space=pltpu.SMEM)
    own, mine = call(
        cut_body, "cut", (array(BF16, rows, cols), array(BF16, rows // 4, cols)), (jnp.stack([core, x]), proj_weight), first=scalars
    )
    grouped, token = call(
        regroup_body, "regroup", (array(BF16, 8, PIECE, KV), TOKEN), (replica_params[0],), (mine,),
        scratch=[pltpu.VMEM((ROWS, KV), F32), pltpu.VMEM((8, PIECE, KV), F32)],
    )
    grouped = lax.all_to_all(grouped, ("x", "core"), 0, 0)
    mirror = [(2 * z + h, 2 * (7 - z) + 1 - h) for z in range(8) for h in range(2)]
    other = lax.ppermute(mine, ("z_lo", "z_hi"), mirror)
    own_next = exchange(own, "y", False)
    normed = norm(hidden_in, norm_gain.reshape(1, -1), token)
    pieces, token, normed = call(
        first_sum_body, "first_sum", (array(F32, 8, 56, LANES), TOKEN), (grouped,), (other, own_next),
        scratch=[pltpu.VMEM((PIECE, KV), F32)], through=normed,
    )
    pieces = lax.all_to_all(pieces, "z_lo", 0, 0)
    (early,) = call(lay_body, "pair", (array(BF16, 2, rows, cols),), (own, own_next), (token,))
    late = exchange(early, "y", True)
    (other,) = call(hold_body, "hold", (array(BF16, *other.shape),), (other,), (token,), cost=LONG)
    others = [other] + spread(other, "y")
    delta, squares, token, normed = call(
        second_sum_body, "second_sum", (array(F32, *share), array(F32, 32, 8, LANES), TOKEN),
        (pieces, outer_params), others[1:], [pltpu.VMEM((56, LANES), F32)], through=normed,
    )
    squares = lax.all_to_all(squares, ("y", "x", "core"), 0, 0)
    ys, other_ys, xs = order_of(y, core), [(y - s) % 4 for s in (0,) + SHIFTS], order_of(x, core)
    order = jnp.stack([2 * k + half for k in ys] + [2 * k + 1 - half for k in other_ys] + xs)
    quad = call(lay_body, "lay", (array(BF16, 4, rows // 4, cols),), others, (token,), cost=LONG)[0]
    quad_next = exchange(quad, "x", False)
    far_normed = lax.ppermute(normed, "core", swap)
    squares, token = call(
        spread_sum_body, "spread_sum", (array(F32, 16, 8, LANES), TOKEN), (squares,), (quad_next,)
    )
    squares = lax.all_to_all(squares, ("z_lo", "z_hi"), 0, 0)
    quads = call(lay_body, "pair", (array(BF16, 2, 4, rows // 4, cols),), (quad, quad_next), (token,))[0]
    quad_late = exchange(quads, "x", True)
    sums, kept = project_own(order, normed, far_normed, early, late, token)
    near, far = call(
        project_other_body, "project_other", (array(BF16, normed.shape[0], cols),) * 2,
        (order, kept, quad, quad_next, quad_late, sums),
        first=scalars, scratch=[pltpu.VMEM((4, rows, cols), BF16)], cost=LONG,
    )
    far = lax.ppermute(far, "core", swap)
    new_outer, new_momentum, projected = call(
        finish_body, "finish", (array(F32, *share), array(F32, *share), array(BF16, near.shape[0], KV)),
        (core.reshape(1), squares, delta, outer_params, momentum, near, far), first=scalars,
    )
    return (projected, new_outer, new_momentum)


def solution(mesh):
    inner = Mesh(mesh.devices.reshape(SIZES), NAMES)
    replica, fsdp = NAMES[:3], NAMES[3:]
    in_specs = (
        P(replica + fsdp, None),
        P(),
        P(fsdp, None),
        P(replica, fsdp, None),
        P(fsdp + replica, None),
        P(fsdp + replica, None),
    )
    out_specs = (
        P(replica + fsdp, None),
        P(fsdp + replica, None),
        P(fsdp + replica, None),
    )
    return jax.shard_map(
        on_device, mesh=inner, in_specs=in_specs, out_specs=out_specs, check_vma=False
    )
```
